256 devices in a mesh: tensor: 2 (over x_lo), node: 16 (over x_hi, z), local: 8 (over y, core).
Axes of the slice: x: 4 (x_hi: 2, x_lo: 2; x = x_hi * 2 + x_lo), y: 4, z: 8, core: 2. Of those that a mesh axis runs over, the one named last changes fastest.
Arguments:
- acts: bfloat16 [16384, 6144], P(('node', 'local')), may hold values from -0.1875 to 0.1875
- grad_q: bfloat16 [16384, 6144], P(('node', 'local'), 'tensor'), may hold values from -6 to 6
- weight_q: bfloat16 [6144, 6144], P('local', 'tensor'), may hold values from -0.078125 to 0.078125
Outputs:
- weight_grad: float32 [8, 768, 6144], P('local', 'node', 'tensor')
- act_grad: bfloat16 [16384, 6144], P(('node', 'local'))
The draws below stay inside these ranges and needn't reach their ends.
All inputs are finite; a program needn't handle non-finite values.
Results may differ from the reference program's by a relative error of at most 0.001.
Values may be sent and summed in bfloat16 or wider, within the bound.
A program may use at most 128 MiB of HBM per device.

```python
import jax
import jax.numpy as jnp
from jax import lax

D = 6144
TOK_DEV = 128
QW = 6144
TOKENS = 16384
N_NODE = 16
N_LOCAL = 8


def with_spikes(array, rng, source, target, parts, factor):
    owner, partner = [(jnp.arange(array.shape[position]) // (array.shape[position] // parts)).reshape([-1 if axis == position else 1 for axis in range(array.ndim)]) for position in (source, target)]
    chosen = jax.random.permutation(rng, parts)[partner]
    strong = (owner == chosen) | (owner == (partner + parts // 2) % parts)
    return jnp.where(strong, factor * array, array)


def block_scale(rng, dims, pieces, smallest, high):
    def one(position, shards_of):
        draws = jax.random.uniform(jax.random.fold_in(jax.random.fold_in(rng, 6), position), (shards_of,), jnp.float32, smallest / len(pieces), high / len(pieces))
        return jnp.repeat(jnp.exp(draws), dims[position] // shards_of).reshape((-1,) + (1,) * (len(dims) - position - 1))

    gain = one(*pieces[0])
    for cut in pieces[1:]:
        gain = gain * one(*cut)
    return gain


def gaussian(stream_key, shape, spread, most, cuts=(), held_as=jnp.bfloat16):
    loudness = block_scale(stream_key, shape, cuts, -0.22, 0.18) if cuts else 1.0
    drawn = jax.random.normal(stream_key, shape, jnp.float32) * spread * loudness
    return jnp.minimum(jnp.maximum(drawn, -most), most).astype(held_as)


def bell_draw_with(rng, extent, spread, bound, shards, heavy, kind=jnp.bfloat16):
    values = spread * jax.random.normal(rng, extent, jnp.float32)
    if shards:
        values = values * block_scale(rng, extent, shards, -0.22, 0.18)
    return jnp.clip(with_spikes(values, jax.random.fold_in(rng, 3), *heavy), -bound, bound).astype(kind)


def setup_inputs(seed: int = 0) -> dict:
    seeds = jax.random.split(jax.random.key(seed), 4)
    return {
        "acts": bell_draw_with(seeds[0], (TOKENS, D), (TOKENS ** -0.5), 0.1875, ((0, 128),), (0, 1, 128, 5.5)),
        "grad_q": gaussian(seeds[1], (TOKENS, QW), 1.0, 6.0, ((0, 128), (1, 2))),
        "weight_q": gaussian(seeds[2], (D, QW), QW ** -0.5, 0.078125, ((0, 8), (1, 2))),
    }


def reference(acts, grad_q, weight_q):
    group = N_LOCAL * TOK_DEV
    grouped_acts = acts.reshape(N_NODE, group, D)
    grouped_grads = grad_q.reshape(N_NODE, group, QW)

    def accumulate(total, pair):
        part = jnp.dot(pair[0].T, pair[1], preferred_element_type=jnp.float32)
        return total + part, None

    full_grad, unused = lax.scan(accumulate, jnp.zeros((D, QW), jnp.float32), (grouped_acts, grouped_grads))
    weight_grad = full_grad.reshape(N_LOCAL, D // N_LOCAL, QW)
    act_grad = jnp.dot(grad_q, weight_q.T, preferred_element_type=jnp.float32).astype(jnp.bfloat16)
    return weight_grad, act_grad
```

```python
import functools

import jax
import jax.numpy as jnp
from jax import lax
from jax.experimental import pallas as pl
from jax.experimental.pallas import tpu as pltpu
from jax.sharding import PartitionSpec as P

MESH = pl.DeviceIdType.MESH
F32, BF16 = jnp.float32, jnp.bfloat16

TOK = 128
D_BLK = 768
HALF = 384
QL = 3072
CW = 768
NK = QL // CW
ROWS = 48
NU = 2 * NK

Z_SCALE = 128.0
X_SCALE = 64.0


def power_code(v, scale):
    v = v * scale
    v2 = v * v
    v4 = v2 * v2
    return (v4 * v2 * v).astype(BF16)


def power_value(code, scale):
    c = code.astype(F32)
    root = jnp.exp(jnp.log(jnp.maximum(jnp.abs(c), 1e-38)) * (1.0 / 7.0)) * (1.0 / scale)
    root = jnp.where(jnp.abs(c) < 1e-37, 0.0, root)
    return jnp.where(c < 0, -root, root)


def kernel(
    acts, grads, wq, wg_out, ag_out,
    W, G, A, AT, PZ, PX, zs, zr, xs, xr, hs, hr, fin,
    loc_sem, sib_sem, a_ss, a_rs, g_ss, g_rs, z_ss, z_rs, x_ss, x_rs, h_ss, h_rs,
    o_ss, o_rs, ag_ss, ag_rs,
):
    t = lax.axis_index("tensor")
    n = lax.axis_index("node")
    l = lax.axis_index("local")
    xh, z = n // 8, n % 8
    y, c = l // 2, l % 2
    yp, ym, y2 = (y + 1) % 4, (y + 3) % 4, (y + 2) % 4

    def at_local(l_):
        return (t, n, l_)

    sib = at_local(y * 2 + 1 - c)
    dev_yp, dev_ym = at_local(yp * 2 + c), at_local(ym * 2 + c)
    dev_z = (
        (t, xh * 8 + (z + 1) % 8, l),
        (t, xh * 8 + (z + 7) % 8, l),
    )
    dev_h = (t, (1 - xh) * 8 + z, l)
    dev_x = (1 - t, n, l)

    started = []

    def send(src, dst, ss, rs, dev):
        cp = pltpu.make_async_remote_copy(
            src_ref=src, dst_ref=dst, send_sem=ss, recv_sem=rs, device_id=dev, device_id_type=MESH
        )
        cp.start()
        started.append(cp)

    def arrived(dst, rs):
        pltpu.make_async_remote_copy(
            src_ref=dst, dst_ref=dst, send_sem=rs, recv_sem=rs, device_id=sib, device_id_type=MESH
        ).wait_recv()

    barrier = pltpu.get_barrier_semaphore()
    partners = [at_local((l + o) % 8) for o in range(1, 8)] + [dev_z[0], dev_z[1], dev_h, dev_x]
    for dev in partners:
        pl.semaphore_signal(barrier, inc=1, device_id=dev, device_id_type=MESH)
    pl.semaphore_wait(barrier, len(partners))

    def cols(k):
        return pl.ds(k * CW, CW)

    def acts_cols(l_, hf):
        h = (1 - xh) if hf == 0 else xh
        return pl.ds(pl.multiple_of(l_ * D_BLK + h * HALF, 128), HALF)

    def out_cols(l_, t_):
        return pl.ds(pl.multiple_of(l_ * D_BLK + t_ * HALF, 128), HALF)

    local = [
        pltpu.make_async_copy(grads, G.at[l], loc_sem.at[0]),
        pltpu.make_async_copy(wq, W, loc_sem.at[1]),
        pltpu.make_async_copy(acts.at[:, acts_cols(l, 0)], A.at[0, l], loc_sem.at[2]),
        pltpu.make_async_copy(acts.at[:, acts_cols(l, 1)], A.at[1, l], loc_sem.at[3]),
    ]

    def send_acts(hf):
        for o in (4, 5, 3, 2, 6, 7, 1):
            l_ = (l + o) % 8
            send(acts.at[:, acts_cols(l_, hf)], A.at[hf, l], a_ss.at[hf, o], a_rs.at[hf, o], at_local(l_))

    def take_acts(hf):
        for o in range(1, 8):
            arrived(A.at[hf, (l + 8 - o) % 8], a_rs.at[hf, o])
        for i in range(8):
            AT[hf, :, i * TOK : (i + 1) * TOK] = A[hf, i].T

    def send_own(k):
        src = grads.at[:, cols(k)]
        send(src, G.at[l, :, cols(k)], g_ss.at[k, 0], g_rs.at[k, 0], dev_yp)
        send(src, G.at[l, :, cols(k)], g_ss.at[k, 1], g_rs.at[k, 1], dev_ym)

    def relay(k):
        lm, lp = ym * 2 + c, yp * 2 + c
        below, above = G.at[lm, :, cols(k)], G.at[lp, :, cols(k)]
        arrived(below, g_rs.at[k, 0])
        low = G.at[lm, pl.ds(0, TOK // 2), cols(k)]
        send(low, low, g_ss.at[k, 2], g_rs.at[k, 2], dev_yp)
        arrived(above, g_rs.at[k, 1])
        high = G.at[lp, pl.ds(TOK // 2, TOK // 2), cols(k)]
        send(high, high, g_ss.at[k, 3], g_rs.at[k, 3], dev_ym)
        send(below, below, g_ss.at[k, 4], g_rs.at[k, 4], sib)
        send(above, above, g_ss.at[k, 5], g_rs.at[k, 5], sib)

    def complete(k):
        lf = y2 * 2 + c
        arrived(G.at[lf, pl.ds(0, TOK // 2), cols(k)], g_rs.at[k, 2])
        arrived(G.at[lf, pl.ds(TOK // 2, TOK // 2), cols(k)], g_rs.at[k, 3])
        far = G.at[lf, :, cols(k)]
        send(far, far, g_ss.at[k, 6], g_rs.at[k, 6], sib)
        arrived(G.at[ym * 2 + 1 - c, :, cols(k)], g_rs.at[k, 4])
        arrived(G.at[yp * 2 + 1 - c, :, cols(k)], g_rs.at[k, 5])
        arrived(G.at[y2 * 2 + 1 - c, :, cols(k)], g_rs.at[k, 6])

    def unit_block(u):
        hf, k = divmod(u, NK)

        @pl.loop(0, CW // 256)
        def _(i):
            at = pl.multiple_of(k * CW + i * 256, 128)
            g = G[:, :, pl.ds(at, 256)].reshape(8 * TOK, 256)
            PZ[u, :, pl.ds(pl.multiple_of(i * 256, 128), 256)] = jnp.dot(
                AT[hf], g, preferred_element_type=F32
            )

    def steps_of(u, d):
        return (1, 2, 3, 4) if u % 2 == d else (2, 3, 4)

    def z_step(u, s):
        for d in range(2):
            if s not in steps_of(u, d):
                continue
            first = s == steps_of(u, d)[0]
            to = (z + 5 - s) % 8 if d == 0 else (z + 3 + s) % 8
            if not first:
                arrived(zr.at[u, d, s - 2], z_rs.at[u, d, s - 2])

            @pl.loop(0, ROWS // 16)
            def _(i):
                r = pl.ds(pl.multiple_of(i * 16, 16), 16)
                v = PZ[u, pl.ds(pl.multiple_of(to * ROWS + i * 16, 16), 16), :]
                if not first:
                    v = v + power_value(zr[u, d, s - 2, r, :], Z_SCALE)
                zs[u, d, s - 1, r, :] = power_code(v, Z_SCALE)

            send(zs.at[u, d, s - 1], zr.at[u, d, s - 1], z_ss.at[u, d, s - 1], z_rs.at[u, d, s - 1], dev_z[d])

    def z_final(u):
        hf, k = divmod(u, NK)
        for d in range(2):
            arrived(zr.at[u, d, 3], z_rs.at[u, d, 3])
        if hf == 1:
            arrived(hr.at[k], h_rs.at[k])

        @pl.loop(0, ROWS // 16)
        def _(i):
            r = pl.ds(pl.multiple_of(i * 16, 16), 16)
            v = PZ[u, pl.ds(pl.multiple_of(z * ROWS + i * 16, 16), 16), :]
            v = v + power_value(zr[u, 0, 3, r, :], Z_SCALE) + power_value(zr[u, 1, 3, r, :], Z_SCALE)
            if hf == 0:
                hs[k, r, :] = power_code(v, Z_SCALE)
            else:
                wg_out[0, r, cols(k)] = v + power_value(hr[k, r, :], Z_SCALE)

        if hf == 0:
            send(hs.at[k], hr.at[k], h_ss.at[k], h_rs.at[k], dev_h)

    chip = (y, yp, ym, y2)

    def x_add(b, k, first):
        yb = chip[b]

        @pl.loop(0, 2)
        def _(i):
            g = G[yb * 2 + i, :, cols(k)]
            p = lax.dot_general(g, W[:, cols(k)], (((1,), (1,)), ((), ())), preferred_element_type=F32)
            r = pl.ds(pl.multiple_of(i * TOK, TOK), TOK)
            PX[b, r, :] = p if first else PX[b, r, :] + p

    def x_send(b):
        theirs = pl.ds(pl.multiple_of((1 - t) * HALF, 128), HALF)

        @pl.loop(0, 2 * TOK // 32)
        def _(i):
            r = pl.ds(pl.multiple_of(i * 32, 32), 32)
            xs[b, r, :] = power_code(PX[b, r, theirs], X_SCALE)

        send(xs.at[b], xr.at[b], x_ss.at[b], x_rs.at[b], dev_x)

    def x_final(b):
        arrived(xr.at[b], x_rs.at[b])
        mine = pl.ds(pl.multiple_of(t * HALF, 128), HALF)

        @pl.loop(0, 2 * TOK // 32)
        def _(i):
            r = pl.ds(pl.multiple_of(i * 32, 32), 32)
            fin[b, r, :] = (PX[b, r, mine] + power_value(xr[b, r, :], X_SCALE)).astype(BF16)

        if b == 0:
            own = pl.ds(pl.multiple_of(c * TOK, TOK), TOK)
            other = pl.ds(pl.multiple_of((1 - c) * TOK, TOK), TOK)
            cp = pltpu.make_async_copy(fin.at[0, own], ag_out.at[:, out_cols(l, t)], loc_sem.at[4])
            cp.start()
            local.append(cp)
            send(fin.at[0, own], ag_out.at[:, out_cols(l, t)], ag_ss.at[0], ag_rs.at[0], dev_x)
            send(fin.at[0, other], ag_out.at[:, out_cols(l, t)], o_ss.at[0], o_rs.at[1], sib)
        else:
            for i in range(2):
                there = {1: 2, 2: 1, 3: 3}[b]
                send(
                    fin.at[b, pl.ds(i * TOK, TOK)], ag_out.at[:, out_cols(l, t)],
                    o_ss.at[2 * b + i], o_rs.at[2 * there + c], at_local(chip[b] * 2 + i),
                )

    def x_share(b):
        for i in range(2):
            if b == 0 and i == 0:
                continue
            l_ = (y * 2 + 1 - c) if b == 0 else chip[b] * 2 + i
            piece = ag_out.at[:, out_cols(l_, t)]
            arrived(piece, o_rs.at[2 * b + i])
            send(piece, piece, ag_ss.at[2 * b + i], ag_rs.at[2 * b + i], dev_x)

    local[0].start()
    local[1].start()
    send(grads, G.at[l], sib_sem.at[0], sib_sem.at[1], sib)
    send_own(0)
    local[2].start()
    send_acts(0)
    local[3].start()
    local[0].wait()
    local[1].wait()
    arrived(G.at[y * 2 + 1 - c], sib_sem.at[1])
    for k in range(NK):
        x_add(0, k, k == 0)
    x_send(0)
    relay(0)
    send_own(1)
    x_final(0)
    local[2].wait()
    take_acts(0)
    complete(0)
    for slot in range(NU + 5):
        u = slot
        if u < NK:
            if u + 2 < NK:
                send_own(u + 2)
            if u == 2:
                send_acts(1)
        if u == NK:
            local[3].wait()
            take_acts(1)
        if u < NU:
            unit_block(u)
            z_step(u, 1)
        if u < NK:
            if u + 1 < NK:
                relay(u + 1)
            for b in (1, 2, 3):
                x_add(b, u, u == 0)
                if u == NK - 1:
                    x_send(b)
        for s in (2, 3, 4):
            if 0 <= u - (s - 1) < NU:
                z_step(u - (s - 1), s)
        if 0 <= u - 4 < NU:
            z_final(u - 4)
        if u == 0:
            x_share(0)
        if u + 1 < NK:
            complete(u + 1)
        if u == NK:
            for b in (1, 2, 3):
                x_final(b)
        if u == NK + 1:
            for b in (1, 2, 3):
                x_share(b)
    for b in range(4):
        for i in range(2):
            l_ = (l if i == 0 else y * 2 + 1 - c) if b == 0 else chip[b] * 2 + i
            arrived(ag_out.at[:, out_cols(l_, 1 - t)], ag_rs.at[2 * b + i])
    local[4].wait()
    for cp in started:
        cp.wait_send()


def on_device(acts, grad_q, weight_q):
    dma = pltpu.SemaphoreType.DMA
    return pl.pallas_call(
        kernel,
        out_shape=(
            jax.ShapeDtypeStruct((1, ROWS, QL), F32),
            jax.ShapeDtypeStruct((TOK, 8 * D_BLK), BF16),
        ),
        in_specs=[pl.BlockSpec(memory_space=pl.ANY)] * 3,
        out_specs=(pl.BlockSpec(memory_space=pltpu.VMEM), pl.BlockSpec(memory_space=pl.ANY)),
        scratch_shapes=[
            pltpu.VMEM((D_BLK, QL), BF16),
            pltpu.VMEM((8, TOK, QL), BF16),
            pltpu.VMEM((2, 8, TOK, HALF), BF16),
            pltpu.VMEM((2, HALF, 8 * TOK), BF16),
            pltpu.VMEM((NU, HALF, CW), F32),
            pltpu.VMEM((4, 2 * TOK, D_BLK), F32),
            pltpu.VMEM((NU, 2, 4, ROWS, CW), BF16),
            pltpu.VMEM((NU, 2, 4, ROWS, CW), BF16),
            pltpu.VMEM((4, 2 * TOK, HALF), BF16),
            pltpu.VMEM((4, 2 * TOK, HALF), BF16),
            pltpu.VMEM((NK, ROWS, CW), BF16),
            pltpu.VMEM((NK, ROWS, CW), BF16),
            pltpu.VMEM((4, 2 * TOK, HALF), BF16),
            dma((5,)),
            dma((2,)),
            dma((2, 8)),
            dma((2, 8)),
            dma((NK, 7)),
            dma((NK, 7)),
            dma((NU, 2, 4)),
            dma((NU, 2, 4)),
            dma((4,)),
            dma((4,)),
            dma((NK,)),
            dma((NK,)),
            dma((8,)),
            dma((8,)),
            dma((8,)),
            dma((8,)),
        ],
        compiler_params=pltpu.CompilerParams(
            collective_id=0, has_side_effects=True, vmem_limit_bytes=56 * 2**20
        ),
        name="projection_backward",
    )(acts, grad_q, weight_q)


def solution(mesh):
    placed = (P(("node", "local"), None), P(("node", "local"), "tensor"), P("local", "tensor"))
    return jax.shard_map(
        on_device,
        mesh=mesh,
        in_specs=placed,
        out_specs=(P("local", "node", "tensor"), P(("node", "local"), None)),
        check_vma=False,
    )
```

```python
import jax
import jax.numpy as jnp
from jax import lax
from jax.experimental import pallas as pl
from jax.experimental.pallas import tpu as pltpu
from jax.sharding import PartitionSpec as P

MESH = pl.DeviceIdType.MESH
F32, BF16 = jnp.float32, jnp.bfloat16

TOK = 128
D_BLK = 768
HALF = 384
QL = 3072
CW = 768
NK = QL // CW
ROWS = 48
NU = 2 * NK

A_NEAR = 80
A_FAR = TOK - A_NEAR

Z_POWER, Z_SCALE = 5, 1024.0
X_POWER, X_TOP = 15, 300.0


def power(v, p):
    out, square = None, v
    while p:
        if p & 1:
            out = square if out is None else out * square
        p >>= 1
        if p:
            square = square * square
    return out


def root(code, p):
    a = jnp.abs(code)
    r = jnp.exp(jnp.log(jnp.maximum(a, 1e-38)) * (1.0 / p))
    r = jnp.where(a < 1e-37, 0.0, r)
    return jnp.where(code < 0, -r, r)


def z_code(v):
    return power(v * Z_SCALE, Z_POWER).astype(BF16)


def z_value(code):
    return root(code.astype(F32), Z_POWER) * (1.0 / Z_SCALE)


def kernel(
    acts, grads, wq, wg_out, ag_out,
    W, G, AS, A, AT, PZ, PX, zs, zr, xs, xr, hs, hr, wo, fin, AO,
    lg_sem, lw_sem, la_sem, lo_sem, lz_sem, sib_sem, a_ss, a_rs, ax_ss, ax_rs, g_ss, g_rs,
    z_ss, z_rs, x_ss, x_rs, h_ss, h_rs, o_ss, o_rs, ag_ss, ag_rs,
):
    t = lax.axis_index("tensor")
    n = lax.axis_index("node")
    l = lax.axis_index("local")
    xh, z = n // 8, n % 8
    y, c = l // 2, l % 2
    yp, ym, y2 = (y + 1) % 4, (y + 3) % 4, (y + 2) % 4
    chip = (y, yp, ym, y2)

    def at_local(l_):
        return (t, n, l_)

    l_sib = y * 2 + 1 - c
    sib = at_local(l_sib)
    dev_yp, dev_ym = at_local(yp * 2 + c), at_local(ym * 2 + c)
    dev_z = (
        (t, xh * 8 + (z + 1) % 8, l),
        (t, xh * 8 + (z + 7) % 8, l),
    )
    dev_h = (t, (1 - xh) * 8 + z, l)
    dev_x = (1 - t, n, l)

    started, stores = [], []

    def send(src, dst, ss, rs, dev):
        cp = pltpu.make_async_remote_copy(
            src_ref=src, dst_ref=dst, send_sem=ss, recv_sem=rs, device_id=dev, device_id_type=MESH
        )
        cp.start()
        started.append(cp)

    def arrived(dst, rs):
        pltpu.make_async_remote_copy(
            src_ref=dst, dst_ref=dst, send_sem=rs, recv_sem=rs, device_id=sib, device_id_type=MESH
        ).wait_recv()

    def store(src, dst, sem):
        cp = pltpu.make_async_copy(src, dst, sem)
        cp.start()
        stores.append(cp)

    def cols(k):
        return pl.ds(k * CW, CW)

    def acts_cols(l_, hf):
        h = (1 - xh) if hf == 0 else xh
        return pl.ds(pl.multiple_of(l_ * D_BLK + h * HALF, 128), HALF)

    def out_cols(l_, t_):
        return pl.ds(pl.multiple_of(l_ * D_BLK + t_ * HALF, 128), HALF)

    load_g = [pltpu.make_async_copy(grads.at[:, cols(k)], G.at[k, l], lg_sem.at[k]) for k in range(NK)]
    load_w = pltpu.make_async_copy(wq, W, lw_sem.at[0])
    far_first = (4, 5, 3, 2, 6, 7, 1, 0)
    load_a = [
        [
            pltpu.make_async_copy(
                acts.at[:, acts_cols((l + o) % 8, hf)], AS.at[hf, (l + o) % 8], la_sem.at[hf, o]
            )
            for o in far_first
        ]
        for hf in range(2)
    ]

    load_g[0].start()
    for cp in load_a[0]:
        cp.start()
    for cp in load_g[1:]:
        cp.start()
    load_w.start()
    for cp in load_a[1]:
        cp.start()

    barrier = pltpu.get_barrier_semaphore()
    partners = [at_local((l + o) % 8) for o in range(1, 8)] + [dev_z[0], dev_z[1], dev_h, dev_x]
    for dev in partners:
        pl.semaphore_signal(barrier, inc=1, device_id=dev, device_id_type=MESH)
    pl.semaphore_wait(barrier, len(partners))

    def a_rows(first, size):
        return pl.ds(pl.multiple_of(first, 16), size)

    order = ((2, 0), (2, 1), (1, 0), (3, 0), (1, 1), (3, 1))

    def peer(off, flip, sign):
        yy = (y + off) % 4 if sign > 0 else (y + 4 - off) % 4
        return yy * 2 + (1 - c if flip else c)

    def send_acts(hf):
        for cp in load_a[hf]:
            cp.wait()
        for i, (off, flip) in enumerate(order):
            l_ = peer(off, flip, 1)
            r = a_rows(t * A_FAR, A_NEAR)
            send(AS.at[hf, l_, r], A.at[hf, l, r], a_ss.at[hf, i], a_rs.at[hf, i], at_local(l_))
        send(AS.at[hf, l_sib], A.at[hf, l], a_ss.at[hf, 6], a_rs.at[hf, 6], sib)

    def pass_acts(hf):
        for i, (off, flip) in enumerate(order):
            l_ = peer(off, flip, -1)
            arrived(A.at[hf, l_, a_rows(t * A_FAR, A_NEAR)], a_rs.at[hf, i])
            r = a_rows(t * A_NEAR, A_FAR)
            send(A.at[hf, l_, r], A.at[hf, l_, r], ax_ss.at[hf, i], ax_rs.at[hf, i], dev_x)

    def take_acts(hf):
        arrived(A.at[hf, l_sib], a_rs.at[hf, 6])
        for i, (off, flip) in enumerate(order):
            arrived(A.at[hf, peer(off, flip, -1), a_rows((1 - t) * A_NEAR, A_FAR)], ax_rs.at[hf, i])
        A[hf, l] = AS[hf, l]
        for i in range(8):
            AT[hf, :, i * TOK : (i + 1) * TOK] = A[hf, i].T

    def send_own(k):
        send(G.at[k, l], G.at[k, l], g_ss.at[k, 0], g_rs.at[k, 0], dev_yp)
        send(G.at[k, l], G.at[k, l], g_ss.at[k, 1], g_rs.at[k, 1], dev_ym)

    def relay(k):
        lm, lp = ym * 2 + c, yp * 2 + c
        low, high = pl.ds(0, TOK // 2), pl.ds(TOK // 2, TOK // 2)
        arrived(G.at[k, lm], g_rs.at[k, 0])
        send(G.at[k, lm, low], G.at[k, lm, low], g_ss.at[k, 2], g_rs.at[k, 2], dev_yp)
        arrived(G.at[k, lp], g_rs.at[k, 1])
        send(G.at[k, lp, high], G.at[k, lp, high], g_ss.at[k, 3], g_rs.at[k, 3], dev_ym)
        send(G.at[k, lm], G.at[k, lm], g_ss.at[k, 4], g_rs.at[k, 4], sib)
        send(G.at[k, lp], G.at[k, lp], g_ss.at[k, 5], g_rs.at[k, 5], sib)

    def near(k):
        arrived(G.at[k, ym * 2 + 1 - c], g_rs.at[k, 4])
        arrived(G.at[k, yp * 2 + 1 - c], g_rs.at[k, 5])

    def far(k):
        lf = y2 * 2 + c
        arrived(G.at[k, lf, pl.ds(0, TOK // 2)], g_rs.at[k, 2])
        arrived(G.at[k, lf, pl.ds(TOK // 2, TOK // 2)], g_rs.at[k, 3])
        send(G.at[k, lf], G.at[k, lf], g_ss.at[k, 6], g_rs.at[k, 6], sib)
        arrived(G.at[k, y2 * 2 + 1 - c], g_rs.at[k, 6])

    def unit_block(u):
        k, hf = divmod(u, 2)

        @pl.loop(0, CW // 256)
        def _(i):
            at = pl.ds(pl.multiple_of(i * 256, 128), 256)
            g = G[k, :, :, at].reshape(8 * TOK, 256)
            PZ[u, :, at] = jnp.dot(AT[hf], g, preferred_element_type=F32)

    def steps_of(u, d):
        return (1, 2, 3, 4) if u % 2 == d else (2, 3, 4)

    def z_step(u, s):
        if not 0 <= u < NU:
            return
        for d in range(2):
            if s not in steps_of(u, d):
                continue
            first = s == steps_of(u, d)[0]
            to = (z + 5 - s) % 8 if d == 0 else (z + 3 + s) % 8
            if not first:
                arrived(zr.at[u, d, s - 2], z_rs.at[u, d, s - 2])

            @pl.loop(0, ROWS // 16)
            def _(i):
                r = pl.ds(pl.multiple_of(i * 16, 16), 16)
                v = PZ[u, pl.ds(pl.multiple_of(to * ROWS + i * 16, 16), 16), :]
                if not first:
                    v = v + z_value(zr[u, d, s - 2, r, :])
                zs[u, d, s - 1, r, :] = z_code(v)

            send(zs.at[u, d, s - 1], zr.at[u, d, s - 1], z_ss.at[u, d, s - 1], z_rs.at[u, d, s - 1], dev_z[d])

    def z_final(u):
        if not 0 <= u < NU:
            return
        k, hf = divmod(u, 2)
        for d in range(2):
            arrived(zr.at[u, d, 3], z_rs.at[u, d, 3])
        if hf == 1:
            arrived(hr.at[k], h_rs.at[k])

        @pl.loop(0, ROWS // 16)
        def _(i):
            r = pl.ds(pl.multiple_of(i * 16, 16), 16)
            v = PZ[u, pl.ds(pl.multiple_of(z * ROWS + i * 16, 16), 16), :]
            v = v + z_value(zr[u, 0, 3, r, :]) + z_value(zr[u, 1, 3, r, :])
            if hf == 0:
                hs[k, r, :] = z_code(v)
            else:
                wo[k, r, :] = v + z_value(hr[k, r, :])

        if hf == 0:
            send(hs.at[k], hr.at[k], h_ss.at[k], h_rs.at[k], dev_h)
        else:
            store(wo.at[k], wg_out.at[0, :, cols(k)], lz_sem.at[k])

    def x_add(b, k):
        yb = chip[b]

        @pl.loop(0, 2)
        def _(i):
            p = lax.dot_general(
                G[k, yb * 2 + i], W[:, cols(k)], (((1,), (1,)), ((), ())), preferred_element_type=F32
            )
            r = pl.ds(pl.multiple_of(i * TOK, TOK), TOK)
            PX[b, r, :] = p if k == 0 else PX[b, r, :] + p

    NB = 2 * TOK

    def x_send(b):
        theirs = pl.ds(pl.multiple_of((1 - t) * HALF, 128), HALF)
        most = jnp.zeros((32, HALF), F32)
        for i in range(NB // 32):
            most = jnp.maximum(most, jnp.abs(PX[b, pl.ds(i * 32, 32), theirs]))
        most = jnp.maximum(jnp.max(most, axis=0, keepdims=True) * 1.01, 1e-30).astype(BF16)
        xs[b, pl.ds(NB, 16), :] = jnp.broadcast_to(most, (16, HALF))
        scale = X_TOP / most.astype(F32)

        @pl.loop(0, NB // 32)
        def _(i):
            r = pl.ds(pl.multiple_of(i * 32, 32), 32)
            xs[b, r, :] = power(PX[b, r, theirs] * scale, X_POWER).astype(BF16)

        send(xs.at[b], xr.at[b], x_ss.at[b], x_rs.at[b], dev_x)

    def x_final(b):
        arrived(xr.at[b], x_rs.at[b])
        mine = pl.ds(pl.multiple_of(t * HALF, 128), HALF)
        unscale = xr[b, pl.ds(NB, 16), :].astype(F32)[0:1] * (1.0 / X_TOP)

        @pl.loop(0, NB // 32)
        def _(i):
            r = pl.ds(pl.multiple_of(i * 32, 32), 32)
            v = PX[b, r, mine] + root(xr[b, r, :].astype(F32), X_POWER) * unscale
            fin[b, r, :] = v.astype(BF16)

        if b == 0:
            own = fin.at[0, pl.ds(pl.multiple_of(c * TOK, TOK), TOK)]
            other = fin.at[0, pl.ds(pl.multiple_of((1 - c) * TOK, TOK), TOK)]
            store(own, ag_out.at[:, out_cols(l, t)], lo_sem.at[0, 0])
            send(own, AO.at[t, l], ag_ss.at[0], ag_rs.at[0], dev_x)
            send(other, AO.at[t, l], o_ss.at[0], o_rs.at[1], sib)
        else:
            there = {1: 2, 2: 1, 3: 3}[b]
            for i in range(2):
                send(
                    fin.at[b, pl.ds(i * TOK, TOK)], AO.at[t, l],
                    o_ss.at[2 * b + i], o_rs.at[2 * there + c], at_local(chip[b] * 2 + i),
                )

    def x_share(b):
        for i in range(2):
            if b == 0 and i == 0:
                continue
            l_ = l_sib if b == 0 else chip[b] * 2 + i
            piece = AO.at[t, l_]
            arrived(piece, o_rs.at[2 * b + i])
            send(piece, piece, ag_ss.at[2 * b + i], ag_rs.at[2 * b + i], dev_x)
            store(piece, ag_out.at[:, out_cols(l_, t)], lo_sem.at[0, 2 * b + i])

    def x_take(b):
        for i in range(2):
            l_ = (l if i == 0 else l_sib) if b == 0 else chip[b] * 2 + i
            piece = AO.at[1 - t, l_]
            arrived(piece, ag_rs.at[2 * b + i])
            store(piece, ag_out.at[:, out_cols(l_, 1 - t)], lo_sem.at[1, 2 * b + i])

    load_g[0].wait()
    send_own(0)
    send_acts(0)
    for cp in load_g[1:]:
        cp.wait()
    send(G.at[:, l], G.at[:, l], sib_sem.at[0], sib_sem.at[1], sib)
    load_w.wait()
    arrived(G.at[:, l_sib], sib_sem.at[1])
    for k in range(NK):
        x_add(0, k)
    x_send(0)
    relay(0)
    send_own(1)
    pass_acts(0)
    send_acts(1)
    near(0)
    x_final(0)
    take_acts(0)
    far(0)
    for u in range(NU + 4):
        k, hf = divmod(u, 2)
        if hf == 0 and k + 2 < NK:
            send_own(k + 2)
        if u < NU:
            unit_block(u)
            z_step(u, 1)
        if u == 0:
            pass_acts(1)
        if hf == 0 and k + 1 < NK:
            relay(k + 1)
        if hf == 0 and k < NK - 1:
            for b in (1, 2, 3):
                x_add(b, k)
        if hf == 1 and k + 1 < NK:
            near(k + 1)
            if k + 1 == NK - 1:
                for b in (1, 2):
                    x_add(b, NK - 1)
                    x_send(b)
        z_step(u - 1, 2)
        if u == 0:
            take_acts(1)
        z_step(u - 2, 3)
        if hf == 1 and k + 1 < NK:
            far(k + 1)
            if k + 1 == NK - 1:
                x_add(3, NK - 1)
                x_send(3)
        z_step(u - 3, 4)
        z_final(u - 4)
        if u == 1:
            x_share(0)
        if u == NU - 2:
            x_final(1)
            x_final(2)
        if u == NU - 1:
            x_final(3)
            x_share(1)
            x_share(2)
        if u == NU:
            x_share(3)
            x_take(0)
    for b in (1, 2, 3):
        x_take(b)
    for cp in stores:
        cp.wait()
    for cp in started:
        cp.wait_send()


def on_device(acts, grad_q, weight_q):
    dma = pltpu.SemaphoreType.DMA
    return pl.pallas_call(
        kernel,
        out_shape=(
            jax.ShapeDtypeStruct((1, ROWS, QL), F32),
            jax.ShapeDtypeStruct((TOK, 8 * D_BLK), BF16),
        ),
        in_specs=[pl.BlockSpec(memory_space=pl.ANY)] * 3,
        out_specs=[pl.BlockSpec(memory_space=pl.ANY)] * 2,
        scratch_shapes=[
            pltpu.VMEM((D_BLK, QL), BF16),
            pltpu.VMEM((NK, 8, TOK, CW), BF16),
            pltpu.VMEM((2, 8, TOK, HALF), BF16),
            pltpu.VMEM((2, 8, TOK, HALF), BF16),
            pltpu.VMEM((2, HALF, 8 * TOK), BF16),
            pltpu.VMEM((NU, HALF, CW), F32),
            pltpu.VMEM((4, 2 * TOK, D_BLK), F32),
            pltpu.VMEM((NU, 2, 4, ROWS, CW), BF16),
            pltpu.VMEM((NU, 2, 4, ROWS, CW), BF16),
            pltpu.VMEM((4, 2 * TOK + 16, HALF), BF16),
            pltpu.VMEM((4, 2 * TOK + 16, HALF), BF16),
            pltpu.VMEM((NK, ROWS, CW), BF16),
            pltpu.VMEM((NK, ROWS, CW), BF16),
            pltpu.VMEM((NK, ROWS, CW), F32),
            pltpu.VMEM((4, 2 * TOK, HALF), BF16),
            pltpu.VMEM((2, 8, TOK, HALF), BF16),
            dma((NK,)),
            dma((1,)),
            dma((2, 8)),
            dma((2, 8)),
            dma((NK,)),
            dma((2,)),
            dma((2, 7)),
            dma((2, 7)),
            dma((2, 6)),
            dma((2, 6)),
            dma((NK, 7)),
            dma((NK, 7)),
            dma((NU, 2, 4)),
            dma((NU, 2, 4)),
            dma((4,)),
            dma((4,)),
            dma((NK,)),
            dma((NK,)),
            dma((8,)),
            dma((8,)),
            dma((8,)),
            dma((8,)),
        ],
        compiler_params=pltpu.CompilerParams(
            collective_id=0, has_side_effects=True, vmem_limit_bytes=58 * 2**20
        ),
        name="projection_backward",
    )(acts, grad_q, weight_q)


def solution(mesh):
    placed = (P(("node", "local"), None), P(("node", "local"), "tensor"), P("local", "tensor"))
    return jax.shard_map(
        on_device,
        mesh=mesh,
        in_specs=placed,
        out_specs=(P("local", "node", "tensor"), P(("node", "local"), None)),
        check_vma=False,
    )
```

```python
import jax
import jax.numpy as jnp
from jax import lax
from jax.experimental import pallas as pl
from jax.experimental.pallas import tpu as pltpu
from jax.sharding import PartitionSpec as P

MESH = pl.DeviceIdType.MESH
F32, BF16 = jnp.float32, jnp.bfloat16

TOK = 128
D_BLK = 768
HALF = 384
QL = 3072
WIDTHS = (384, 768, 768, 768, 384)
FIRST = tuple(sum(WIDTHS[:k]) for k in range(len(WIDTHS)))
NK = len(WIDTHS)
ROWS = 48
UNITS = ((0, 0), (1, 0), (0, 1), (1, 1), (2, 0), (2, 1), (3, 0), (4, 0), (3, 1), (4, 1))
NU = len(UNITS)

A_NEAR = 80
A_FAR = TOK - A_NEAR

Z_POWER, Z_SCALE = 5, 1024.0
X_POWER, X_TOP = 15, 300.0


def power(v, p):
    out, square = None, v
    while p:
        if p & 1:
            out = square if out is None else out * square
        p >>= 1
        if p:
            square = square * square
    return out


def root(code, p):
    a = jnp.abs(code)
    r = jnp.exp(jnp.log(jnp.maximum(a, 1e-38)) * (1.0 / p))
    r = jnp.where(a < 1e-37, 0.0, r)
    return jnp.where(code < 0, -r, r)


def z_code(v):
    return power(v * Z_SCALE, Z_POWER).astype(BF16)


def z_value(code):
    return root(code.astype(F32), Z_POWER) * (1.0 / Z_SCALE)


def kernel(
    acts, grads, wq, wg_out, ag_out,
    W, G, AS, A, AT, PZ, PX, zs, zr, xs, xr, hs, hr, wo, fin, AO,
    lg_sem, lw_sem, la_sem, lo_sem, lz_sem, sib_rs, a_ss, a_rs, ax_rs, g_ss, g_rs,
    z_ss, z_rs, x_ss, x_rs, h_ss, h_rs, o_ss, o_rs, ag_ss, ag_rs,
):
    t = lax.axis_index("tensor")
    n = lax.axis_index("node")
    l = lax.axis_index("local")
    xh, z = n // 8, n % 8
    y, c = l // 2, l % 2
    yp, ym, y2 = (y + 1) % 4, (y + 3) % 4, (y + 2) % 4
    chip = (y, yp, ym, y2)

    def at_local(l_):
        return (t, n, l_)

    l_sib = y * 2 + 1 - c
    sib = at_local(l_sib)
    dev_yp, dev_ym = at_local(yp * 2 + c), at_local(ym * 2 + c)
    dev_z = (
        (t, xh * 8 + (z + 1) % 8, l),
        (t, xh * 8 + (z + 7) % 8, l),
    )
    dev_h = (t, (1 - xh) * 8 + z, l)
    dev_x = (1 - t, n, l)


    def send(src, dst, ss, rs, dev):
        cp = pltpu.make_async_remote_copy(
            src_ref=src, dst_ref=dst, send_sem=ss, recv_sem=rs, device_id=dev, device_id_type=MESH
        )
        cp.start()

    def arrived(dst, rs):
        pltpu.make_async_remote_copy(
            src_ref=dst, dst_ref=dst, send_sem=rs, recv_sem=rs, device_id=sib, device_id_type=MESH
        ).wait_recv()

    def sent(total, ss):
        pltpu.make_async_remote_copy(
            src_ref=total, dst_ref=total, send_sem=ss, recv_sem=ss, device_id=sib, device_id_type=MESH
        ).wait_send()

    def store(src, dst, sem):
        pltpu.make_async_copy(src, dst, sem).start()

    def cols(k):
        return pl.ds(FIRST[k], WIDTHS[k])

    def acts_cols(l_, hf):
        h = (1 - xh) if hf == 0 else xh
        return pl.ds(pl.multiple_of(l_ * D_BLK + h * HALF, 128), HALF)

    def out_cols(l_, t_):
        return pl.ds(pl.multiple_of(l_ * D_BLK + t_ * HALF, 128), HALF)

    load_g = [pltpu.make_async_copy(grads.at[:, cols(k)], G[k].at[l], lg_sem.at[k]) for k in range(NK)]
    load_w = pltpu.make_async_copy(wq, W, lw_sem.at[0])
    far_first = (4, 5, 3, 2, 6, 7, 1, 0)
    load_a = [
        [
            pltpu.make_async_copy(
                acts.at[:, acts_cols((l + o) % 8, hf)], AS.at[hf, (l + o) % 8], la_sem.at[hf]
            )
            for o in far_first
        ]
        for hf in range(2)
    ]

    load_g[0].start()
    for cp in load_a[0]:
        cp.start()
    for cp in load_g[1:]:
        cp.start()
    load_w.start()
    for cp in load_a[1]:
        cp.start()

    barrier = pltpu.get_barrier_semaphore()
    partners = [at_local((l + o) % 8) for o in range(1, 8)] + [dev_z[0], dev_z[1], dev_h, dev_x]
    for dev in partners:
        pl.semaphore_signal(barrier, inc=1, device_id=dev, device_id_type=MESH)
    pl.semaphore_wait(barrier, len(partners))

    def a_rows(first, size):
        return pl.ds(pl.multiple_of(first, 16), size)

    order = ((2, 0), (2, 1), (1, 0), (3, 0), (1, 1), (3, 1))

    def peer(off, flip, sign):
        yy = (y + off) % 4 if sign > 0 else (y + 4 - off) % 4
        return yy * 2 + (1 - c if flip else c)

    def send_acts(hf, part):
        if part == 0:
            pltpu.make_async_copy(AS.at[hf], AS.at[hf], la_sem.at[hf]).wait()
        for i, (off, flip) in list(enumerate(order))[3 * part : 3 * part + 3]:
            l_ = peer(off, flip, 1)
            r = a_rows(t * A_FAR, A_NEAR)
            send(AS.at[hf, l_, r], A.at[hf, l, r], a_ss.at[hf], a_rs.at[hf, i], at_local(l_))
        if part == 0:
            send(AS.at[hf, l_sib], A.at[hf, l], a_ss.at[hf], a_rs.at[hf, 6], sib)

    def pass_acts(hf):
        for i, (off, flip) in enumerate(order):
            l_ = peer(off, flip, -1)
            arrived(A.at[hf, l_, a_rows(t * A_FAR, A_NEAR)], a_rs.at[hf, i])
            r = a_rows(t * A_NEAR, A_FAR)
            send(A.at[hf, l_, r], A.at[hf, l_, r], a_ss.at[hf], ax_rs.at[hf, i], dev_x)

    def turn(hf, l_, block):
        AT[hf, :, pl.ds(pl.multiple_of(l_ * TOK, TOK), TOK)] = block.T

    def take_acts(hf):
        turn(hf, l, AS[hf, l])
        arrived(A.at[hf, l_sib], a_rs.at[hf, 6])
        turn(hf, l_sib, A[hf, l_sib])
        for i, (off, flip) in enumerate(order):
            l_ = peer(off, flip, -1)
            arrived(A.at[hf, l_, a_rows((1 - t) * A_NEAR, A_FAR)], ax_rs.at[hf, i])
            turn(hf, l_, A[hf, l_])

    def send_own(k):
        own = G[k].at[l]
        send(own, own, g_ss.at[k], g_rs.at[k, 0], dev_yp)
        send(own, own, g_ss.at[k], g_rs.at[k, 1], dev_ym)

    def relay(k):
        lm, lp = ym * 2 + c, yp * 2 + c
        below, above = G[k].at[lm], G[k].at[lp]
        low, high = G[k].at[lm, pl.ds(0, TOK // 2)], G[k].at[lp, pl.ds(TOK // 2, TOK // 2)]
        arrived(below, g_rs.at[k, 0])
        send(low, low, g_ss.at[k], g_rs.at[k, 2], dev_yp)
        arrived(above, g_rs.at[k, 1])
        send(high, high, g_ss.at[k], g_rs.at[k, 3], dev_ym)
        send(below, below, g_ss.at[k], g_rs.at[k, 4], sib)
        send(above, above, g_ss.at[k], g_rs.at[k, 5], sib)

    def near(k):
        arrived(G[k].at[ym * 2 + 1 - c], g_rs.at[k, 4])
        arrived(G[k].at[yp * 2 + 1 - c], g_rs.at[k, 5])

    def far(k):
        lf = y2 * 2 + c
        arrived(G[k].at[lf, pl.ds(0, TOK // 2)], g_rs.at[k, 2])
        arrived(G[k].at[lf, pl.ds(TOK // 2, TOK // 2)], g_rs.at[k, 3])
        send(G[k].at[lf], G[k].at[lf], g_ss.at[k], g_rs.at[k, 6], sib)
        arrived(G[k].at[y2 * 2 + 1 - c], g_rs.at[k, 6])

    def send_shard():
        for k in range(NK):
            if k:
                load_g[k].wait()
            send(G[k].at[l], G[k].at[l], g_ss.at[k], sib_rs.at[k], sib)

    def take_shard():
        for k in range(NK):
            arrived(G[k].at[l_sib], sib_rs.at[k])

    def unit_block(u):
        k, hf = UNITS[u]

        tile = 384

        @pl.loop(0, WIDTHS[k] // tile)
        def _(i):
            at = pl.ds(pl.multiple_of(i * tile, 128), tile)
            g = G[k][:, :, at].reshape(8 * TOK, tile)
            PZ[u][:, at] = jnp.dot(AT[hf], g, preferred_element_type=F32)

    def steps_of(u, d):
        return (1, 2, 3, 4) if u % 2 == d else (2, 3, 4)

    def z_slot(u, d, s):
        return s - 1 if u % 2 == d else s + 2

    def z_step(u, s):
        if not 0 <= u < NU:
            return
        for d in range(2):
            if s not in steps_of(u, d):
                continue
            first = s == steps_of(u, d)[0]
            to = (z + 5 - s) % 8 if d == 0 else (z + 3 + s) % 8
            last, now = z_slot(u, d, s - 1), z_slot(u, d, s)
            if not first:
                arrived(zr[u].at[last], z_rs.at[u, last])

            @pl.loop(0, ROWS // 16)
            def _(i):
                r = pl.ds(pl.multiple_of(i * 16, 16), 16)
                v = PZ[u][pl.ds(pl.multiple_of(to * ROWS + i * 16, 16), 16), :]
                if not first:
                    v = v + z_value(zr[u][last, r, :])
                zs[u][now, r, :] = z_code(v)

            send(zs[u].at[now], zr[u].at[now], z_ss.at[u], z_rs.at[u, now], dev_z[d])

    def z_final(u):
        if not 0 <= u < NU:
            return
        k, hf = UNITS[u]
        low, high = z_slot(u, 0, 4), z_slot(u, 1, 4)
        arrived(zr[u].at[low], z_rs.at[u, low])
        arrived(zr[u].at[high], z_rs.at[u, high])
        if hf == 1:
            arrived(hr[k], h_rs.at[k])

        @pl.loop(0, ROWS // 16)
        def _(i):
            r = pl.ds(pl.multiple_of(i * 16, 16), 16)
            v = PZ[u][pl.ds(pl.multiple_of(z * ROWS + i * 16, 16), 16), :]
            v = v + z_value(zr[u][low, r, :]) + z_value(zr[u][high, r, :])
            if hf == 0:
                hs[k][r, :] = z_code(v)
            else:
                wo[k][r, :] = v + z_value(hr[k][r, :])

        if hf == 0:
            send(hs[k], hr[k], h_ss.at[k], h_rs.at[k], dev_h)
        else:
            store(wo[k], wg_out.at[0, :, cols(k)], lz_sem.at[k])

    def x_add(b, k):
        yb = chip[b]

        g = G[k][pl.ds(yb * 2, 2)].reshape(2 * TOK, WIDTHS[k])
        p = lax.dot_general(g, W[:, cols(k)], (((1,), (1,)), ((), ())), preferred_element_type=F32)
        PX[b] = p if k == 0 else PX[b] + p

    NB = 2 * TOK

    def x_send(b):
        theirs = pl.ds(pl.multiple_of((1 - t) * HALF, 128), HALF)
        most = jnp.zeros((32, HALF), F32)
        for i in range(NB // 32):
            most = jnp.maximum(most, jnp.abs(PX[b, pl.ds(i * 32, 32), theirs]))
        most = jnp.maximum(jnp.max(most, axis=0, keepdims=True) * 1.01, 1e-30).astype(BF16)
        xs[b, pl.ds(NB, 16), :] = jnp.broadcast_to(most, (16, HALF))
        scale = X_TOP / most.astype(F32)

        @pl.loop(0, NB // 32)
        def _(i):
            r = pl.ds(pl.multiple_of(i * 32, 32), 32)
            xs[b, r, :] = power(PX[b, r, theirs] * scale, X_POWER).astype(BF16)

        send(xs.at[b], xr.at[b], x_ss.at[0], x_rs.at[b], dev_x)

    def x_final(b):
        arrived(xr.at[b], x_rs.at[b])
        mine = pl.ds(pl.multiple_of(t * HALF, 128), HALF)
        unscale = xr[b, pl.ds(NB, 16), :].astype(F32)[0:1] * (1.0 / X_TOP)

        @pl.loop(0, NB // 32)
        def _(i):
            r = pl.ds(pl.multiple_of(i * 32, 32), 32)
            v = PX[b, r, mine] + root(xr[b, r, :].astype(F32), X_POWER) * unscale
            fin[b, r, :] = v.astype(BF16)

        if b == 0:
            own = fin.at[0, pl.ds(pl.multiple_of(c * TOK, TOK), TOK)]
            other = fin.at[0, pl.ds(pl.multiple_of((1 - c) * TOK, TOK), TOK)]
            store(own, ag_out.at[:, out_cols(l, t)], lo_sem.at[0])
            send(own, AO.at[t, l], ag_ss.at[0], ag_rs.at[0], dev_x)
            send(other, AO.at[t, l], o_ss.at[0], o_rs.at[1], sib)
        else:
            there = {1: 2, 2: 1, 3: 3}[b]
            for i in range(2):
                send(
                    fin.at[b, pl.ds(i * TOK, TOK)], AO.at[t, l],
                    o_ss.at[0], o_rs.at[2 * there + c], at_local(chip[b] * 2 + i),
                )

    def x_share(b):
        for i in range(2):
            if b == 0 and i == 0:
                continue
            l_ = l_sib if b == 0 else chip[b] * 2 + i
            piece = AO.at[t, l_]
            arrived(piece, o_rs.at[2 * b + i])
            send(piece, piece, ag_ss.at[0], ag_rs.at[2 * b + i], dev_x)
            store(piece, ag_out.at[:, out_cols(l_, t)], lo_sem.at[0])

    def x_take(b):
        for i in range(2):
            l_ = (l if i == 0 else l_sib) if b == 0 else chip[b] * 2 + i
            piece = AO.at[1 - t, l_]
            arrived(piece, ag_rs.at[2 * b + i])
            store(piece, ag_out.at[:, out_cols(l_, 1 - t)], lo_sem.at[0])

    load_g[0].wait()
    send_own(0)
    send_acts(0, 0)
    send_acts(0, 1)
    send_shard()
    relay(0)
    send_own(1)
    pass_acts(0)
    load_w.wait()
    take_shard()
    for i in range(NK):
        x_add(0, i)
    send_acts(1, 0)
    send_acts(1, 1)
    near(0)
    far(0)
    take_acts(0)
    unit_block(0)
    z_step(0, 1)
    relay(1)
    send_own(2)
    x_send(0)
    near(1)
    far(1)
    send_own(3)
    unit_block(1)
    z_step(1, 1)
    z_step(0, 2)
    pass_acts(1)
    x_final(0)
    relay(2)
    send_own(4)
    for b in (1, 2, 3):
        x_add(b, 0)
        x_add(b, 1)
    relay(3)
    take_acts(1)
    unit_block(2)
    z_step(2, 1)
    z_step(1, 2)
    z_step(0, 3)
    unit_block(3)
    z_step(3, 1)
    near(2)
    far(2)
    unit_block(4)
    z_step(4, 1)
    relay(4)
    z_step(2, 2)
    z_step(1, 3)
    unit_block(5)
    z_step(5, 1)
    z_step(0, 4)
    for b in (1, 2, 3):
        x_add(b, 2)
    z_step(3, 2)
    near(3)
    far(3)
    near(4)
    far(4)
    x_add(1, 3)
    x_add(1, 4)
    x_send(1)
    unit_block(6)
    z_step(6, 1)
    x_add(2, 3)
    x_add(2, 4)
    x_send(2)
    z_step(2, 3)
    z_step(1, 4)
    x_add(3, 3)
    x_add(3, 4)
    x_send(3)
    z_step(4, 2)
    z_step(3, 3)
    z_final(0)
    unit_block(7)
    z_step(7, 1)
    z_step(5, 2)
    z_step(2, 4)
    z_final(1)
    z_step(4, 3)
    z_step(3, 4)
    x_final(1)
    unit_block(8)
    z_step(8, 1)
    z_step(6, 2)
    z_step(5, 3)
    z_step(4, 4)
    x_share(0)
    x_final(2)
    unit_block(9)
    z_step(9, 1)
    z_step(7, 2)
    x_share(1)
    z_step(6, 3)
    z_step(5, 4)
    z_final(4)
    x_final(3)
    z_step(8, 2)
    z_step(9, 2)
    x_share(2)
    z_step(7, 3)
    z_step(6, 4)
    z_step(8, 3)
    z_step(9, 3)
    x_share(3)
    z_step(7, 4)
    z_final(2)
    z_final(3)
    z_step(8, 4)
    z_final(6)
    z_step(9, 4)
    z_final(7)
    z_final(5)
    x_take(0)
    x_take(1)
    x_take(2)
    x_take(3)
    z_final(8)
    z_final(9)
    for k in range(NK):
        pltpu.make_async_copy(wo[k], wg_out.at[0, :, cols(k)], lz_sem.at[k]).wait()
        sent(G[k].at[pl.ds(0, 7)], g_ss.at[k])
        sent(hs[k], h_ss.at[k])
    for hf in range(2):
        sent(A.at[hf, pl.ds(0, 7)], a_ss.at[hf])
    for u in range(NU):
        sent(zs[u], z_ss.at[u])
    sent(xs, x_ss.at[0])
    sent(AO.at[0, pl.ds(0, 7)], o_ss.at[0])
    sent(AO.at[0], ag_ss.at[0])
    pltpu.make_async_copy(AO, AO, lo_sem.at[0]).wait()


def move(a, b, out_a, out_b, va, vb, sems):
    steps = []
    for src, mid, dst, sem in (
        *((a.at[:, :, pl.ds(i * 1536, 1536)], va.at[:, :, pl.ds(i * 1536, 1536)], out_a.at[:, :, pl.ds(i * 1536, 1536)], i) for i in range(2)),
        *((b.at[pl.ds(i * 32, 32)], vb.at[pl.ds(i * 32, 32)], out_b.at[pl.ds(i * 32, 32)], 2 + i) for i in range(4)),
    ):
        steps.append((pltpu.make_async_copy(src, mid, sems.at[0, sem]), pltpu.make_async_copy(mid, dst, sems.at[1, sem])))
    for read, _ in steps:
        read.start()
    for read, write in steps:
        read.wait()
        write.start()
    for _, write in steps:
        write.wait()


def on_device(acts, grad_q, weight_q):
    dma = pltpu.SemaphoreType.DMA
    vmem = pltpu.VMEM
    units = [WIDTHS[k] for k, _ in UNITS]
    outs = (
        jax.ShapeDtypeStruct((1, ROWS, QL), F32),
        jax.ShapeDtypeStruct((TOK, 8 * D_BLK), BF16),
    )
    anywhere = pl.BlockSpec(memory_space=pl.ANY)
    results = pl.pallas_call(
        kernel,
        out_shape=outs,
        in_specs=[anywhere] * 3,
        out_specs=[anywhere] * 2,
        scratch_shapes=[
            vmem((D_BLK, QL), BF16),
            [vmem((8, TOK, w), BF16) for w in WIDTHS],
            vmem((2, 8, TOK, HALF), BF16),
            vmem((2, 8, TOK, HALF), BF16),
            vmem((2, HALF, 8 * TOK), BF16),
            [vmem((HALF, w), F32) for w in units],
            vmem((4, 2 * TOK, D_BLK), F32),
            [vmem((7, ROWS, w), BF16) for w in units],
            [vmem((7, ROWS, w), BF16) for w in units],
            vmem((4, 2 * TOK + 16, HALF), BF16),
            vmem((4, 2 * TOK + 16, HALF), BF16),
            [vmem((ROWS, w), BF16) for w in WIDTHS],
            [vmem((ROWS, w), BF16) for w in WIDTHS],
            [vmem((ROWS, w), F32) for w in WIDTHS],
            vmem((4, 2 * TOK, HALF), BF16),
            vmem((2, 8, TOK, HALF), BF16),
            dma((NK,)),
            dma((1,)),
            dma((2,)),
            dma((1,)),
            dma((NK,)),
            dma((NK,)),
            dma((2,)),
            dma((2, 7)),
            dma((2, 6)),
            dma((NK,)),
            dma((NK, 7)),
            dma((NU,)),
            dma((NU, 7)),
            dma((1,)),
            dma((4,)),
            dma((NK,)),
            dma((NK,)),
            dma((1,)),
            dma((8,)),
            dma((1,)),
            dma((8,)),
        ],
        compiler_params=pltpu.CompilerParams(
            collective_id=0, has_side_effects=True, vmem_limit_bytes=58 * 2**20
        ),
        name="projection_backward",
    )(acts, grad_q, weight_q)
    return pl.pallas_call(
        move,
        out_shape=outs,
        in_specs=[anywhere] * 2,
        out_specs=[anywhere] * 2,
        scratch_shapes=[vmem(outs[0].shape, F32), vmem(outs[1].shape, BF16), dma((2, 6))],
        name="results",
    )(*results)


def solution(mesh):
    placed = (P(("node", "local"), None), P(("node", "local"), "tensor"), P("local", "tensor"))
    return jax.shard_map(
        on_device,
        mesh=mesh,
        in_specs=placed,
        out_specs=(P("local", "node", "tensor"), P(("node", "local"), None)),
        check_vma=False,
    )
```

```python
import jax
import jax.numpy as jnp
from jax import lax
from jax.experimental import pallas as pl
from jax.experimental.pallas import tpu as pltpu
from jax.sharding import PartitionSpec as P

MESH = pl.DeviceIdType.MESH
F32, BF16 = jnp.float32, jnp.bfloat16

TOK = 128
D_BLK = 768
HALF = 384
QL = 3072
WIDTHS = (384, 768, 768, 768, 384)
FIRST = tuple(sum(WIDTHS[:k]) for k in range(len(WIDTHS)))
NK = len(WIDTHS)
ROWS = 48
UNITS = ((0, 0), (1, 0), (0, 1), (1, 1), (2, 0), (2, 1), (3, 0), (4, 0), (3, 1), (4, 1))
NU = len(UNITS)

A_NEAR = 64
A_FAR = TOK - A_NEAR

Z_POWER, Z_SCALE = 5, 1024.0
X_POWER, X_TOP = 15, 300.0


def power(v, p):
    out, square = None, v
    while p:
        if p & 1:
            out = square if out is None else out * square
        p >>= 1
        if p:
            square = square * square
    return out


def root(code, p):
    a = jnp.abs(code)
    r = jnp.exp(jnp.log(jnp.maximum(a, 1e-38)) * (1.0 / p))
    r = jnp.where(a < 1e-37, 0.0, r)
    return jnp.where(code < 0, -r, r)


def z_code(v):
    return power(v * Z_SCALE, Z_POWER).astype(BF16)


def z_value(code):
    return root(code.astype(F32), Z_POWER) * (1.0 / Z_SCALE)


def kernel(
    acts, grads, wq, wg_out, ag_out,
    W, G, AS, A, AT, PZ, PX, zs, zr, xs, xr, hs, hr, wo, fin, AO,
    lg_sem, lw_sem, la_sem, lo_sem, lz_sem, sib_rs, a_ss, a_rs, ax_rs, g_ss, g_rs,
    z_ss, z_rs, x_ss, x_rs, h_ss, h_rs, o_ss, o_rs, ag_ss, ag_rs,
):
    t = lax.axis_index("tensor")
    n = lax.axis_index("node")
    l = lax.axis_index("local")
    xh, z = n // 8, n % 8
    y, c = l // 2, l % 2
    yp, ym, y2 = (y + 1) % 4, (y + 3) % 4, (y + 2) % 4
    chip = (y, yp, ym, y2)

    def at_local(l_):
        return (t, n, l_)

    l_sib = y * 2 + 1 - c
    sib = at_local(l_sib)
    dev_yp, dev_ym = at_local(yp * 2 + c), at_local(ym * 2 + c)
    dev_z = (
        (t, xh * 8 + (z + 1) % 8, l),
        (t, xh * 8 + (z + 7) % 8, l),
    )
    dev_h = (t, (1 - xh) * 8 + z, l)
    dev_x = (1 - t, n, l)


    def send(src, dst, ss, rs, dev):
        cp = pltpu.make_async_remote_copy(
            src_ref=src, dst_ref=dst, send_sem=ss, recv_sem=rs, device_id=dev, device_id_type=MESH
        )
        cp.start()

    def arrived(dst, rs):
        pltpu.make_async_remote_copy(
            src_ref=dst, dst_ref=dst, send_sem=rs, recv_sem=rs, device_id=sib, device_id_type=MESH
        ).wait_recv()

    def sent(total, ss):
        pltpu.make_async_remote_copy(
            src_ref=total, dst_ref=total, send_sem=ss, recv_sem=ss, device_id=sib, device_id_type=MESH
        ).wait_send()

    def store(src, dst, sem):
        pltpu.make_async_copy(src, dst, sem).start()

    def cols(k):
        return pl.ds(FIRST[k], WIDTHS[k])

    def acts_cols(l_, hf):
        h = (1 - xh) if hf == 0 else xh
        return pl.ds(pl.multiple_of(l_ * D_BLK + h * HALF, 128), HALF)

    def out_cols(l_, t_):
        return pl.ds(pl.multiple_of(l_ * D_BLK + t_ * HALF, 128), HALF)

    load_g = [pltpu.make_async_copy(grads.at[:, cols(k)], G[k].at[l], lg_sem.at[k]) for k in range(NK)]
    load_w = pltpu.make_async_copy(wq, W, lw_sem.at[0])
    far_first = (4, 5, 3, 2, 6, 7, 1, 0)
    load_a = [
        [
            pltpu.make_async_copy(
                acts.at[:, acts_cols((l + o) % 8, hf)], AS.at[hf, (l + o) % 8], la_sem.at[hf]
            )
            for o in far_first
        ]
        for hf in range(2)
    ]

    load_g[0].start()
    for cp in load_a[0]:
        cp.start()
    for cp in load_g[1:]:
        cp.start()
    load_w.start()
    for cp in load_a[1]:
        cp.start()

    barrier = pltpu.get_barrier_semaphore()
    partners = [at_local((l + o) % 8) for o in range(1, 8)] + [dev_z[0], dev_z[1], dev_h, dev_x]
    for dev in partners:
        pl.semaphore_signal(barrier, inc=1, device_id=dev, device_id_type=MESH)
    pl.semaphore_wait(barrier, len(partners))

    def a_rows(first, size):
        return pl.ds(pl.multiple_of(first, 16), size)

    order = ((2, 0), (2, 1), (1, 0), (3, 0), (1, 1), (3, 1))

    def peer(off, flip, sign):
        yy = (y + off) % 4 if sign > 0 else (y + 4 - off) % 4
        return yy * 2 + (1 - c if flip else c)

    def send_acts(hf, part):
        if part == 0:
            pltpu.make_async_copy(AS.at[hf], AS.at[hf], la_sem.at[hf]).wait()
        for i, (off, flip) in list(enumerate(order))[3 * part : 3 * part + 3]:
            l_ = peer(off, flip, 1)
            r = a_rows(t * A_FAR, A_NEAR)
            send(AS.at[hf, l_, r], A.at[hf, l, r], a_ss.at[hf], a_rs.at[hf, i], at_local(l_))
        if part == 0:
            send(AS.at[hf, l_sib], A.at[hf, l], a_ss.at[hf], a_rs.at[hf, 6], sib)

    def pass_acts(hf):
        for i, (off, flip) in enumerate(order):
            l_ = peer(off, flip, -1)
            arrived(A.at[hf, l_, a_rows(t * A_FAR, A_NEAR)], a_rs.at[hf, i])
            r = a_rows(t * A_NEAR, A_FAR)
            send(A.at[hf, l_, r], A.at[hf, l_, r], a_ss.at[hf], ax_rs.at[hf, i], dev_x)

    def turn(hf, l_, block):
        AT[hf, :, pl.ds(pl.multiple_of(l_ * TOK, TOK), TOK)] = block.T

    def take_acts(hf):
        turn(hf, l, AS[hf, l])
        arrived(A.at[hf, l_sib], a_rs.at[hf, 6])
        turn(hf, l_sib, A[hf, l_sib])
        for i, (off, flip) in enumerate(order):
            l_ = peer(off, flip, -1)
            arrived(A.at[hf, l_, a_rows((1 - t) * A_NEAR, A_FAR)], ax_rs.at[hf, i])
            turn(hf, l_, A[hf, l_])

    def send_own(k):
        own = G[k].at[l]
        send(own, own, g_ss.at[k], g_rs.at[k, 0], dev_yp)
        send(own, own, g_ss.at[k], g_rs.at[k, 1], dev_ym)

    def relay(k):
        lm, lp = ym * 2 + c, yp * 2 + c
        below, above = G[k].at[lm], G[k].at[lp]
        low, high = G[k].at[lm, pl.ds(0, TOK // 2)], G[k].at[lp, pl.ds(TOK // 2, TOK // 2)]
        arrived(below, g_rs.at[k, 0])
        send(low, low, g_ss.at[k], g_rs.at[k, 2], dev_yp)
        arrived(above, g_rs.at[k, 1])
        send(high, high, g_ss.at[k], g_rs.at[k, 3], dev_ym)
        send(below, below, g_ss.at[k], g_rs.at[k, 4], sib)
        send(above, above, g_ss.at[k], g_rs.at[k, 5], sib)

    def near(k):
        arrived(G[k].at[ym * 2 + 1 - c], g_rs.at[k, 4])
        arrived(G[k].at[yp * 2 + 1 - c], g_rs.at[k, 5])

    def far(k):
        lf = y2 * 2 + c
        arrived(G[k].at[lf, pl.ds(0, TOK // 2)], g_rs.at[k, 2])
        arrived(G[k].at[lf, pl.ds(TOK // 2, TOK // 2)], g_rs.at[k, 3])
        send(G[k].at[lf], G[k].at[lf], g_ss.at[k], g_rs.at[k, 6], sib)
        arrived(G[k].at[y2 * 2 + 1 - c], g_rs.at[k, 6])

    def send_shard():
        for k in range(NK):
            if k:
                load_g[k].wait()
            send(G[k].at[l], G[k].at[l], g_ss.at[k], sib_rs.at[k], sib)

    def take_shard():
        for k in range(NK):
            arrived(G[k].at[l_sib], sib_rs.at[k])

    def unit_block(u):
        k, hf = UNITS[u]

        tile = 384

        @pl.loop(0, WIDTHS[k] // tile)
        def _(i):
            at = pl.ds(pl.multiple_of(i * tile, 128), tile)
            g = G[k][:, :, at].reshape(8 * TOK, tile)
            PZ[u][:, at] = jnp.dot(AT[hf], g, preferred_element_type=F32)

    def steps_of(u, d):
        return (1, 2, 3, 4) if u % 2 == d else (2, 3, 4)

    def z_slot(u, d, s):
        return s - 1 if u % 2 == d else s + 2

    def z_step(u, s):
        if not 0 <= u < NU:
            return
        for d in range(2):
            if s not in steps_of(u, d):
                continue
            first = s == steps_of(u, d)[0]
            to = (z + 5 - s) % 8 if d == 0 else (z + 3 + s) % 8
            last, now = z_slot(u, d, s - 1), z_slot(u, d, s)
            if not first:
                arrived(zr[u].at[last], z_rs.at[u, last])

            @pl.loop(0, ROWS // 16)
            def _(i):
                r = pl.ds(pl.multiple_of(i * 16, 16), 16)
                v = PZ[u][pl.ds(pl.multiple_of(to * ROWS + i * 16, 16), 16), :]
                if not first:
                    v = v + z_value(zr[u][last, r, :])
                zs[u][now, r, :] = z_code(v)

            send(zs[u].at[now], zr[u].at[now], z_ss.at[u], z_rs.at[u, now], dev_z[d])

    def z_final(u):
        if not 0 <= u < NU:
            return
        k, hf = UNITS[u]
        low, high = z_slot(u, 0, 4), z_slot(u, 1, 4)
        arrived(zr[u].at[low], z_rs.at[u, low])
        arrived(zr[u].at[high], z_rs.at[u, high])
        if hf == 1:
            arrived(hr[k], h_rs.at[k])

        @pl.loop(0, ROWS // 16)
        def _(i):
            r = pl.ds(pl.multiple_of(i * 16, 16), 16)
            v = PZ[u][pl.ds(pl.multiple_of(z * ROWS + i * 16, 16), 16), :]
            v = v + z_value(zr[u][low, r, :]) + z_value(zr[u][high, r, :])
            if hf == 0:
                hs[k][r, :] = z_code(v)
            else:
                wo[k][r, :] = v + z_value(hr[k][r, :])

        if hf == 0:
            send(hs[k], hr[k], h_ss.at[k], h_rs.at[k], dev_h)
        else:
            store(wo[k], wg_out.at[0, :, cols(k)], lz_sem.at[k])

    def x_add(b, k):
        yb = chip[b]

        g = G[k][pl.ds(yb * 2, 2)].reshape(2 * TOK, WIDTHS[k])
        p = lax.dot_general(g, W[:, cols(k)], (((1,), (1,)), ((), ())), preferred_element_type=F32)
        PX[b] = p if k == 0 else PX[b] + p

    NB = 2 * TOK

    def x_send(b):
        theirs = pl.ds(pl.multiple_of((1 - t) * HALF, 128), HALF)
        most = jnp.zeros((32, HALF), F32)
        for i in range(NB // 32):
            most = jnp.maximum(most, jnp.abs(PX[b, pl.ds(i * 32, 32), theirs]))
        most = jnp.maximum(jnp.max(most, axis=0, keepdims=True) * 1.01, 1e-30).astype(BF16)
        xs[b, pl.ds(NB, 16), :] = jnp.broadcast_to(most, (16, HALF))
        scale = X_TOP / most.astype(F32)

        @pl.loop(0, NB // 32)
        def _(i):
            r = pl.ds(pl.multiple_of(i * 32, 32), 32)
            xs[b, r, :] = power(PX[b, r, theirs] * scale, X_POWER).astype(BF16)

        send(xs.at[b], xr.at[b], x_ss.at[0], x_rs.at[b], dev_x)

    def x_final(b):
        arrived(xr.at[b], x_rs.at[b])
        mine = pl.ds(pl.multiple_of(t * HALF, 128), HALF)
        unscale = xr[b, pl.ds(NB, 16), :].astype(F32)[0:1] * (1.0 / X_TOP)

        @pl.loop(0, NB // 32)
        def _(i):
            r = pl.ds(pl.multiple_of(i * 32, 32), 32)
            v = PX[b, r, mine] + root(xr[b, r, :].astype(F32), X_POWER) * unscale
            fin[b, r, :] = v.astype(BF16)

        if b == 0:
            own = fin.at[0, pl.ds(pl.multiple_of(c * TOK, TOK), TOK)]
            other = fin.at[0, pl.ds(pl.multiple_of((1 - c) * TOK, TOK), TOK)]
            store(own, ag_out.at[:, out_cols(l, t)], lo_sem.at[0])
            send(own, AO.at[t, l], ag_ss.at[0], ag_rs.at[0], dev_x)
            send(other, AO.at[t, l], o_ss.at[0], o_rs.at[1], sib)
        else:
            there = {1: 2, 2: 1, 3: 3}[b]
            for i in range(2):
                send(
                    fin.at[b, pl.ds(i * TOK, TOK)], AO.at[t, l],
                    o_ss.at[0], o_rs.at[2 * there + c], at_local(chip[b] * 2 + i),
                )

    def x_share(b):
        for i in range(2):
            if b == 0 and i == 0:
                continue
            l_ = l_sib if b == 0 else chip[b] * 2 + i
            piece = AO.at[t, l_]
            arrived(piece, o_rs.at[2 * b + i])
            send(piece, piece, ag_ss.at[0], ag_rs.at[2 * b + i], dev_x)
            store(piece, ag_out.at[:, out_cols(l_, t)], lo_sem.at[0])

    def x_take(b):
        for i in range(2):
            l_ = (l if i == 0 else l_sib) if b == 0 else chip[b] * 2 + i
            piece = AO.at[1 - t, l_]
            arrived(piece, ag_rs.at[2 * b + i])
            store(piece, ag_out.at[:, out_cols(l_, 1 - t)], lo_sem.at[0])

    load_g[0].wait()
    send_own(0)
    send_acts(0, 0)
    send_acts(0, 1)
    send_shard()
    relay(0)
    send_own(1)
    pass_acts(0)
    load_w.wait()
    take_shard()
    for i in range(NK):
        x_add(0, i)
    send_acts(1, 0)
    send_acts(1, 1)
    near(0)
    far(0)
    take_acts(0)
    unit_block(0)
    z_step(0, 1)
    relay(1)
    send_own(2)
    x_send(0)
    near(1)
    far(1)
    send_own(3)
    unit_block(1)
    z_step(1, 1)
    z_step(0, 2)
    pass_acts(1)
    x_final(0)
    relay(2)
    send_own(4)
    for b in (1, 2, 3):
        x_add(b, 0)
        x_add(b, 1)
    relay(3)
    take_acts(1)
    unit_block(2)
    z_step(2, 1)
    z_step(1, 2)
    z_step(0, 3)
    unit_block(3)
    z_step(3, 1)
    relay(4)
    near(2)
    far(2)
    unit_block(4)
    z_step(4, 1)
    z_step(2, 2)
    z_step(1, 3)
    unit_block(5)
    z_step(5, 1)
    z_step(0, 4)
    for b in (1, 2, 3):
        x_add(b, 2)
    z_step(3, 2)
    near(3)
    far(3)
    near(4)
    far(4)
    x_add(1, 3)
    x_add(1, 4)
    x_send(1)
    unit_block(6)
    z_step(6, 1)
    x_add(2, 3)
    x_add(2, 4)
    x_send(2)
    z_step(2, 3)
    z_step(1, 4)
    x_add(3, 3)
    x_add(3, 4)
    x_send(3)
    z_step(4, 2)
    z_step(3, 3)
    z_final(0)
    unit_block(7)
    z_step(7, 1)
    z_step(5, 2)
    z_step(2, 4)
    z_final(1)
    z_step(4, 3)
    z_step(3, 4)
    x_final(1)
    unit_block(8)
    z_step(8, 1)
    z_step(6, 2)
    z_step(5, 3)
    z_step(4, 4)
    x_share(0)
    x_final(2)
    unit_block(9)
    z_step(9, 1)
    z_step(7, 2)
    x_share(1)
    z_step(6, 3)
    z_step(5, 4)
    z_final(4)
    x_final(3)
    z_step(8, 2)
    z_step(9, 2)
    x_share(2)
    z_step(7, 3)
    z_step(6, 4)
    z_step(8, 3)
    z_step(9, 3)
    x_share(3)
    z_step(7, 4)
    z_final(2)
    z_final(3)
    z_step(8, 4)
    z_final(6)
    z_step(9, 4)
    z_final(7)
    z_final(5)
    x_take(0)
    x_take(1)
    x_take(2)
    x_take(3)
    z_final(8)
    z_final(9)
    for k in range(NK):
        pltpu.make_async_copy(wo[k], wg_out.at[0, :, cols(k)], lz_sem.at[k]).wait()
        sent(G[k].at[pl.ds(0, 7)], g_ss.at[k])
        sent(hs[k], h_ss.at[k])
    for hf in range(2):
        sent(A.at[hf, pl.ds(0, 7)], a_ss.at[hf])
    for u in range(NU):
        sent(zs[u], z_ss.at[u])
    sent(xs, x_ss.at[0])
    sent(AO.at[0, pl.ds(0, 7)], o_ss.at[0])
    sent(AO.at[0], ag_ss.at[0])
    pltpu.make_async_copy(AO, AO, lo_sem.at[0]).wait()


def move(a, b, out_a, out_b, va, vb, sems):
    steps = []
    for src, mid, dst, sem in (
        *((a.at[:, :, pl.ds(i * 1536, 1536)], va.at[:, :, pl.ds(i * 1536, 1536)], out_a.at[:, :, pl.ds(i * 1536, 1536)], i) for i in range(2)),
        *((b.at[pl.ds(i * 32, 32)], vb.at[pl.ds(i * 32, 32)], out_b.at[pl.ds(i * 32, 32)], 2 + i) for i in range(4)),
    ):
        steps.append((pltpu.make_async_copy(src, mid, sems.at[0, sem]), pltpu.make_async_copy(mid, dst, sems.at[1, sem])))
    for read, _ in steps:
        read.start()
    for read, write in steps:
        read.wait()
        write.start()
    for _, write in steps:
        write.wait()


def on_device(acts, grad_q, weight_q):
    dma = pltpu.SemaphoreType.DMA
    vmem = pltpu.VMEM
    units = [WIDTHS[k] for k, _ in UNITS]
    outs = (
        jax.ShapeDtypeStruct((1, ROWS, QL), F32),
        jax.ShapeDtypeStruct((TOK, 8 * D_BLK), BF16),
    )
    anywhere = pl.BlockSpec(memory_space=pl.ANY)
    results = pl.pallas_call(
        kernel,
        out_shape=outs,
        in_specs=[anywhere] * 3,
        out_specs=[anywhere] * 2,
        scratch_shapes=[
            vmem((D_BLK, QL), BF16),
            [vmem((8, TOK, w), BF16) for w in WIDTHS],
            vmem((2, 8, TOK, HALF), BF16),
            vmem((2, 8, TOK, HALF), BF16),
            vmem((2, HALF, 8 * TOK), BF16),
            [vmem((HALF, w), F32) for w in units],
            vmem((4, 2 * TOK, D_BLK), F32),
            [vmem((7, ROWS, w), BF16) for w in units],
            [vmem((7, ROWS, w), BF16) for w in units],
            vmem((4, 2 * TOK + 16, HALF), BF16),
            vmem((4, 2 * TOK + 16, HALF), BF16),
            [vmem((ROWS, w), BF16) for w in WIDTHS],
            [vmem((ROWS, w), BF16) for w in WIDTHS],
            [vmem((ROWS, w), F32) for w in WIDTHS],
            vmem((4, 2 * TOK, HALF), BF16),
            vmem((2, 8, TOK, HALF), BF16),
            dma((NK,)),
            dma((1,)),
            dma((2,)),
            dma((1,)),
            dma((NK,)),
            dma((NK,)),
            dma((2,)),
            dma((2, 7)),
            dma((2, 6)),
            dma((NK,)),
            dma((NK, 7)),
            dma((NU,)),
            dma((NU, 7)),
            dma((1,)),
            dma((4,)),
            dma((NK,)),
            dma((NK,)),
            dma((1,)),
            dma((8,)),
            dma((1,)),
            dma((8,)),
        ],
        compiler_params=pltpu.CompilerParams(
            collective_id=0, has_side_effects=True, vmem_limit_bytes=58 * 2**20
        ),
        name="projection_backward",
    )(acts, grad_q, weight_q)
    return pl.pallas_call(
        move,
        out_shape=outs,
        in_specs=[anywhere] * 2,
        out_specs=[anywhere] * 2,
        scratch_shapes=[vmem(outs[0].shape, F32), vmem(outs[1].shape, BF16), dma((2, 6))],
        name="results",
    )(*results)


def solution(mesh):
    placed = (P(("node", "local"), None), P(("node", "local"), "tensor"), P("local", "tensor"))
    return jax.shard_map(
        on_device,
        mesh=mesh,
        in_specs=placed,
        out_specs=(P("local", "node", "tensor"), P(("node", "local"), None)),
        check_vma=False,
    )
```
